32 devices in a mesh: groups: 2 (over y), gy: 16 (over z, x, core), gx: 1.
Axes of the slice: x: 2, y: 2, z: 4, core: 2. Of those that a mesh axis runs over, the one named last changes fastest.
Arguments:
- state: bfloat16 [6, 64, 512, 128], P('groups', None, 'gy', 'gx'), parts along dimension 0, may hold values from -6 to 6
- obs_value: float32 [2048], P(('groups', 'gy', 'gx')), parts along dimension 0, may hold values from -6 to 6
- obs_sigma: float32 [2048], P(('groups', 'gy', 'gx')), parts along dimension 0, may hold values from 0.5 to 2
- obs_pixel: int32 [2048], P(('groups', 'gy', 'gx')), parts along dimension 0, may hold values from 0 to 4095
- obs_route: int32 [2048, 1], P(('groups', 'gy', 'gx')), parts along dimension 0, may hold values from 0 to 15; in each aligned block of 64 rows (0 to 63, 64 to 127, ...) at most 8 rows name the same one
- obs_count: int32 [32], P(('groups', 'gy', 'gx')), parts along dimension 0, may hold values from 32 to 64
- radius: int32 [32, 4], P('groups'), parts along dimension 0, may hold values from 17 to 32
Outputs:
- analysis: bfloat16 [6, 64, 512, 128], P('groups', None, 'gy', 'gx'), parts along dimension 0
The draws below stay inside these ranges and needn't reach their ends.
There are 2 independent parts, one for each index of `groups`. The reference program is written for one: setup_inputs(seed, part) draws one part's arguments, and reference() takes and returns one part's arrays. A program takes and returns all parts, laid end to end along the dimension named above; each array names one. Nothing has to cross between parts.
Inputs may be any that keep to these rules, and one draw needn't show every extreme that they name: `obs_route`: among the 64 slots that arrive at one device, no tile row is named more than 8 times, and in some devices' slots one tile row is named exactly 8 times.
All inputs are finite; a program needn't handle non-finite values.
Results may differ from the reference program's by a relative error of at most 0.0057.
Values may be sent and summed in bfloat16 or wider, within the bound.
A program may use at most 64 MiB of HBM per device.

```python
import math
import jax
import jax.numpy as jnp
import numpy as np
from jax import lax

K = 64
FIELDS = 3
STRIDE = 32
ITER_NS = 6
PR = 1
PC = 4
OBS_DEV = 64
CAP = 8
NPR = 16
NPC = 4
NR = 512
NC = 128
OBS_ALL = 1024
N_GY = 16
N_GX = 1


def place_ends(values, stream_key, low, high):
    longest = values.shape.index(max(values.shape))
    spots = []
    for shift in (0, 1):
        where = [jax.random.randint(jax.random.fold_in(stream_key, axis), (), 0, length) for axis, length in enumerate(values.shape)]
        where[longest] = (where[longest] + shift) % values.shape[longest]
        spots.append(tuple(where))
    return values.at[spots[0]].set(low).at[spots[1]].set(high)


def steps_of(stream_key, extent, cuts, smallest, largest):
    gain = 1.0
    for position, parts in cuts:
        heights = jax.random.uniform(jax.random.fold_in(jax.random.fold_in(stream_key, 6), position), (parts,), jnp.float32, smallest / len(cuts), largest / len(cuts))
        gain = gain * jnp.repeat(jnp.exp(heights), extent[position] // parts).reshape((-1,) + (1,) * (len(extent) - 1 - position))
    return gain


def shared_out(own_key, own, number, rows, count, top, limit, slope):
    order = jax.random.permutation(own_key, count)
    crowded, usual = portions_of(count, rows * top, limit, slope, True), portions_of(count, rows * top, limit, slope, False)
    places = jnp.arange(count)

    def named(tallies, offset_by):
        used = int((tallies > 0).sum())
        fixed = max(1, used // 4)
        shifted = fixed + (places - fixed + offset_by * (used - fixed)) % max(1, count - fixed)
        return jnp.zeros((count,), jnp.int32).at[order[jnp.where(places < fixed, places, shifted)]].set(jnp.asarray(tallies, jnp.int32))

    tallies = jnp.where(number % 4 == 0, named(crowded, number // 4), named(usual, number - number // 4 - 1))
    mixed = jax.random.permutation(jax.random.fold_in(own, 3), count)
    giver, taker = mixed[0:count // 2 * 2:2], mixed[1:count // 2 * 2:2]
    margin = jnp.minimum(tallies[giver] - 1, limit - tallies[taker]) // 2
    margin = jnp.where((giver == order[0]) | (taker == order[0]) | (tallies[taker] == 0), 0, jnp.maximum(margin, 0))
    shifted = jax.random.randint(jax.random.fold_in(own, 4), (count // 2,), 0, 1 << 20) % (margin + 1)
    tallies = tallies.at[giver].add(-shifted).at[taker].add(shifted)
    labels = jnp.searchsorted(jnp.cumsum(tallies), jnp.arange(rows * top), side="right").astype(jnp.int32)
    table = labels.reshape(top, rows).T
    table = table[jax.random.permutation(jax.random.fold_in(own, 1), rows)]
    offset_by = jax.random.randint(jax.random.fold_in(own, 2), (rows, 1), 0, top)
    return jnp.take_along_axis(table, (jnp.arange(top)[None, :] + offset_by) % top, axis=1)


def portions_of(number_of, total, reach, slope, full):
    loads = [(1 << 20) // math.isqrt(grade ** slope) + 1 for grade in range(1, number_of + 1)]
    largest = reach if full else min(reach, max(-(-total // number_of), total * loads[0] // sum(loads)))
    least = 1 if total - largest >= number_of - 1 else 0
    holding, surplus = [largest] + [least] * (number_of - 1), total - largest - least * (number_of - 1)
    while surplus > 0:
        candidates = [i for i in range(1, number_of) if holding[i] < largest] or [i for i in range(1, number_of) if holding[i] < reach]
        pool, budget = sum([loads[i] for i in candidates]), surplus
        for i in candidates:
            extra = min(reach - holding[i], max(1, budget * loads[i] // pool), surplus)
            holding[i] = holding[i] + extra
            surplus = surplus - extra
    return np.array(holding)


def bell_draw(rng, dims, width, bound, split=(), held_as=jnp.bfloat16):
    loudness = steps_of(rng, dims, split, -0.22, 0.18) if split else 1.0
    entries = jax.random.normal(rng, dims, jnp.float32) * width * loudness
    return jnp.minimum(jnp.maximum(entries, -bound), bound).astype(held_as)


def setup_inputs(seed: int = 0, part: int = 0) -> dict:
    key_list = jax.random.split(jax.random.key(seed), 8)
    part_splits = jax.random.split(jax.random.fold_in(key_list[7], part), 8)
    state = bell_draw(part_splits[0], (FIELDS, K, NR, NC), 1.0, 6.0, ((2, 16),))
    obs_value = bell_draw(part_splits[1], (OBS_ALL,), 1.0, 6.0, ((0, 16),), jnp.float32)
    obs_sigma = jnp.clip(jnp.exp(math.log(2.0) - 1.3862944 * jax.random.uniform(part_splits[2], (OBS_ALL,), jnp.float32) ** steps_of(part_splits[2], (OBS_ALL,), ((0, 16),), -0.2, 0.2)), 0.5, 2.0)
    obs_pixel = place_ends(jax.random.randint(part_splits[3], (OBS_ALL,), 0, STRIDE * PR * STRIDE * PC), jax.random.fold_in(part_splits[3], 1), 0, (STRIDE * PR * STRIDE * PC) - 1).astype(jnp.int32)
    obs_route_keys = jax.random.split(jax.random.fold_in(part_splits[4], 1), OBS_ALL // OBS_DEV)
    obs_route_turns = jax.random.permutation(jax.random.fold_in(part_splits[4], 3), OBS_ALL // OBS_DEV)
    obs_route = jax.vmap(lambda own, number: shared_out(jax.random.fold_in(part_splits[4], 2), own, number, OBS_DEV, N_GY, 1, CAP, 2))(obs_route_keys, obs_route_turns).reshape((OBS_ALL, 1))
    obs_count = place_ends(jax.random.randint(part_splits[5], (N_GY * N_GX,), OBS_DEV // 2, OBS_DEV + 1), jax.random.fold_in(part_splits[5], 1), OBS_DEV // 2, OBS_DEV).astype(jnp.int32)
    radius = place_ends(jax.random.randint(part_splits[6], (NPR, NPC), STRIDE // 2 + 1, STRIDE + 1), jax.random.fold_in(part_splits[6], 1), STRIDE // 2 + 1, STRIDE).astype(jnp.int32)
    return {"state": state, "obs_value": obs_value, "obs_sigma": obs_sigma, "obs_pixel": obs_pixel, "obs_route": obs_route, "obs_count": obs_count, "radius": radius}


def obs_operator(values):
    return values[1] * jax.nn.sigmoid(values[0]) - 0.5 * values[2]

def taper_weight(row_offset, col_offset, own_radius):
    distance = row_offset * row_offset + col_offset * col_offset
    squared = own_radius * own_radius
    fraction = distance / squared
    return jnp.where(distance < squared, (1.0 - fraction) * (1.0 - fraction), 0.0)

def solve_weights(gram_matrix, members):
    spread = gram_matrix[..., :members, :]
    forcing = gram_matrix[..., members, :]
    identity = jnp.eye(members, dtype=jnp.float32)
    matrix = identity + spread / (members - 1.0)
    norm_scale = jnp.sqrt(lax.optimization_barrier(jnp.sum(matrix * matrix, axis=(-2, -1), keepdims=True)))
    current = matrix / norm_scale
    inverse_root = jnp.broadcast_to(identity, matrix.shape)
    for iteration in range(ITER_NS):
        factor = 1.5 * identity - 0.5 * jnp.matmul(inverse_root, current, precision=lax.Precision.HIGHEST)
        current = jnp.matmul(current, factor, precision=lax.Precision.HIGHEST)
        inverse_root = jnp.matmul(factor, inverse_root, precision=lax.Precision.HIGHEST)
    square_root = inverse_root / jnp.sqrt(norm_scale)
    pulled = jnp.einsum('...ij,...j->...i', square_root, forcing, precision=lax.Precision.HIGHEST)
    mean_shift = jnp.einsum('...ij,...j->...i', square_root, pulled, precision=lax.Precision.HIGHEST) / (members - 1.0)
    return (square_root + mean_shift[..., :, None]).astype(jnp.bfloat16)

def reference(state, obs_value, obs_sigma, obs_pixel, obs_route, obs_count, radius):
    fields, members, grid_rows, grid_cols = state.shape
    tile_rows = STRIDE * PR
    tile_cols = STRIDE * PC
    half_step = STRIDE // 2
    arrivals = OBS_DEV
    capacity = CAP
    slot_count = capacity * N_GY
    tile_count = N_GY * N_GX
    point_cols = PC * N_GX
    point_rows = PR * N_GY
    block_shape = (N_GY, N_GX, arrivals)
    values = obs_value.reshape(block_shape)
    present = jnp.arange(arrivals)[None, None, :] < obs_count.reshape(N_GY, N_GX)[:, :, None]
    inverse_sigma = jnp.where(present, 1.0 / obs_sigma.reshape(block_shape), 0.0).astype(jnp.float32)
    target_row = obs_route[:, 0].reshape(block_shape)
    pixels = obs_pixel.reshape(block_shape)

    def block_rank(block):
        one_hot = (block[:, None] == jnp.arange(N_GY, dtype=jnp.int32)[None, :]).astype(jnp.int32)
        return lax.optimization_barrier(jnp.sum((jnp.cumsum(one_hot, axis=0) - one_hot) * one_hot, axis=1)).astype(jnp.int32)
    slot_rank = lax.map(block_rank, target_row.reshape(tile_count, arrivals)).reshape(block_shape)
    column_tile = jnp.arange(N_GX, dtype=jnp.int32)[None, :, None]
    source_row = jnp.arange(N_GY, dtype=jnp.int32)[:, None, None]
    global_row = (target_row * tile_rows + pixels // tile_cols).astype(jnp.int32)
    global_col = jnp.broadcast_to(column_tile * tile_cols + pixels % tile_cols, block_shape).astype(jnp.int32)

    def observe(block):
        rows_here, cols_here, value_here, weight_here = block
        picked = state[:, :, rows_here, cols_here].astype(jnp.float32)
        predicted = obs_operator(picked)
        centre = lax.optimization_barrier(jnp.mean(predicted, axis=0))
        spread_rows = ((predicted - centre) * weight_here).astype(jnp.bfloat16)
        misfit = ((value_here - centre) * weight_here).astype(jnp.bfloat16)
        return jnp.concatenate([spread_rows, misfit[None]], axis=0)
    augmented = lax.map(observe, (global_row, global_col, values, inverse_sigma))
    flat_index = ((target_row * N_GX + column_tile) * slot_count + source_row * capacity + slot_rank).reshape(-1).astype(jnp.int32)
    ordered = jnp.moveaxis(augmented, 1, 0).reshape(members + 1, -1)
    tiled = jnp.zeros((members + 1, tile_count * slot_count), jnp.bfloat16).at[:, flat_index].set(ordered)
    tiled = tiled.reshape(members + 1, N_GY, N_GX, slot_count)
    local_spots = jnp.stack([(pixels // tile_cols).astype(jnp.float32), (pixels % tile_cols).astype(jnp.float32)]).reshape(2, -1)
    spots = jnp.zeros((2, tile_count * slot_count), jnp.float32).at[:, flat_index].set(local_spots)
    spots = spots.reshape(2, N_GY, N_GX, slot_count)
    tiled_pad = jnp.pad(tiled, ((0, 0), (1, 1), (0, 0), (0, 0)))
    spots_pad = jnp.pad(spots, ((0, 0), (1, 1), (0, 0), (0, 0)))

    def row_grams(tile_index):
        window = lax.dynamic_slice_in_dim(tiled_pad, tile_index, 3, 1)
        places = lax.dynamic_slice_in_dim(spots_pad, tile_index, 3, 1)
        obs_rows = places[0] + ((jnp.arange(3) - 1) * tile_rows).astype(jnp.float32)[:, None, None]
        obs_cols = places[1] + (jnp.arange(N_GX) * tile_cols).astype(jnp.float32)[None, :, None]
        spreads = window[:members].astype(jnp.float32)

        def point_gram(point_index):
            point_row = point_index // point_cols
            point_col = point_index % point_cols
            centre_row = (STRIDE * point_row + half_step).astype(jnp.float32)
            centre_col = (STRIDE * point_col + half_step).astype(jnp.float32)
            own_radius = radius[tile_index * PR + point_row, point_col].astype(jnp.float32)
            nearness = taper_weight(obs_rows - centre_row, obs_cols - centre_col, own_radius)
            scaled = (nearness[None] * window).astype(jnp.bfloat16).astype(jnp.float32)
            return jnp.einsum('iabs,jabs->ij', scaled, spreads)
        return lax.map(point_gram, jnp.arange(PR * point_cols, dtype=jnp.int32))
    gram_all = lax.map(row_grams, jnp.arange(N_GY, dtype=jnp.int32))
    weights = solve_weights(gram_all, members).reshape(point_rows, point_cols, members, members)
    upper_index = (jnp.arange(2 * PR) + 1) // 2
    left_index = (jnp.arange(2 * point_cols) + 1) // 2
    row_fraction = (((jnp.arange(tile_rows) + half_step) % STRIDE).astype(jnp.float32) / STRIDE).reshape(2 * PR, half_step)
    col_fraction = (((jnp.arange(grid_cols) + half_step) % STRIDE).astype(jnp.float32) / STRIDE).reshape(2 * point_cols, half_step)
    col_pick = jnp.clip(jnp.arange(point_cols + 2) - 1, 0, point_cols - 1)

    def analyse(tile_index):
        block = lax.dynamic_slice_in_dim(state, tile_index * tile_rows, tile_rows, 2).astype(jnp.float32)
        centre_state = lax.optimization_barrier(jnp.mean(block, axis=1))
        anomaly = (block - centre_state[:, None]).astype(jnp.bfloat16)
        row_pick = jnp.clip(tile_index * PR - 1 + jnp.arange(PR + 2), 0, point_rows - 1)
        framed = weights[row_pick][:, col_pick]
        pieces = anomaly.reshape(fields, members, 2 * PR, half_step, 2 * point_cols, half_step).astype(jnp.float32)
        analysis = centre_state.reshape(fields, 1, 2 * PR, half_step, 2 * point_cols, half_step)
        for down_step in (0, 1):
            for right_step in (0, 1):
                corner = framed[upper_index + down_step][:, left_index + right_step].astype(jnp.float32)
                product = jnp.einsum('fkhasb,hskm->fmhasb', pieces, corner)
                row_weight = row_fraction if down_step else 1.0 - row_fraction
                col_weight = col_fraction if right_step else 1.0 - col_fraction
                blend = row_weight[:, :, None, None] * col_weight[None, None]
                analysis = analysis + blend * product
        return analysis.reshape(fields, members, tile_rows, grid_cols).astype(jnp.bfloat16)
    stacked = lax.map(analyse, jnp.arange(N_GY, dtype=jnp.int32))
    return jnp.moveaxis(stacked, 0, 2).reshape(fields, members, grid_rows, grid_cols)
```

```python
import jax
import jax.numpy as jnp
import numpy as np
from jax import lax
from jax.experimental import pallas as pl
from jax.experimental.pallas import tpu as pltpu
from jax.sharding import PartitionSpec as P

STRIDE = 32
ITER_NS = 6
OBS_PEER = 4


def with_halo(cells, sides, width):
    for axis, dim in sides:
        count = lax.axis_size(axis)
        ends = count - 1
        head = lax.slice_in_dim(cells, 0, width, axis=dim)
        tail = lax.slice_in_dim(cells, cells.shape[dim] - width, cells.shape[dim], axis=dim)
        cells = jnp.concatenate(
            [
                lax.ppermute(tail, axis, [(i, (i + 1) % count) for i in range(ends)]),
                cells,
                lax.ppermute(head, axis, [((i + 1) % count, i) for i in range(ends)]),
            ],
            axis=dim,
        )
    return cells


def obs_operator(values):
    return values[1] * jax.nn.sigmoid(values[0]) - 0.5 * values[2]


def taper_weight(row_offset, col_offset, own_radius):
    distance = row_offset * row_offset + col_offset * col_offset
    squared = own_radius * own_radius
    fraction = distance / squared
    return jnp.where(distance < squared, (1.0 - fraction) * (1.0 - fraction), 0.0)


def solve_weights(gram_matrix, members):
    spread = gram_matrix[..., :members, :]
    forcing = gram_matrix[..., members, :]
    identity = jnp.eye(members, dtype=jnp.float32)
    matrix = identity + spread / (members - 1.0)
    norm_scale = jnp.sqrt(jnp.sum(matrix * matrix, axis=(-2, -1), keepdims=True))
    current = matrix / norm_scale
    inverse_root = jnp.broadcast_to(identity, matrix.shape)
    for iteration in range(ITER_NS):
        factor = 1.5 * identity - 0.5 * jnp.matmul(
            inverse_root, current, precision=lax.Precision.HIGHEST
        )
        current = jnp.matmul(current, factor, precision=lax.Precision.HIGHEST)
        inverse_root = jnp.matmul(factor, inverse_root, precision=lax.Precision.HIGHEST)
    square_root = inverse_root / jnp.sqrt(norm_scale)
    pulled = jnp.einsum("...ij,...j->...i", square_root, forcing, precision=lax.Precision.HIGHEST)
    mean_shift = jnp.einsum(
        "...ij,...j->...i", square_root, pulled, precision=lax.Precision.HIGHEST
    ) / (members - 1.0)
    return (square_root + mean_shift[..., :, None]).astype(jnp.bfloat16)


def body(state, obs_value, obs_sigma, obs_pixel, obs_route, obs_count, radius):
    fields, members, tile_rows, tile_cols = state.shape
    row_devices = lax.axis_size("gy")
    col_devices = lax.axis_size("gx")
    row_index = lax.axis_index("gy")
    col_index = lax.axis_index("gx")
    stride = STRIDE
    half_step = stride // 2
    point_rows = tile_rows // stride
    point_cols = tile_cols // stride
    arrivals = obs_value.shape[0]
    capacity = 2 * OBS_PEER
    slot_count = capacity * row_devices
    present = jnp.arange(arrivals) < obs_count[0]
    inverse_sigma = jnp.where(present, 1.0 / obs_sigma, 0.0)
    target_row = obs_route[:, 0]
    one_hot = (target_row[:, None] == jnp.arange(row_devices)[None, :]).astype(jnp.int32)
    slot_rank = jnp.sum((jnp.cumsum(one_hot, axis=0) - one_hot) * one_hot, axis=1)
    placement = target_row * capacity + slot_rank
    record = jnp.stack([obs_value, inverse_sigma, obs_pixel.astype(jnp.float32)])
    outgoing = jnp.zeros((3, slot_count), jnp.float32).at[:, placement].set(record)
    incoming = lax.all_to_all(outgoing, "gy", split_axis=1, concat_axis=1, tiled=True)
    pixels = incoming[2].astype(jnp.int32)
    flattened = state.reshape(fields, members, tile_rows * tile_cols)
    picked = jnp.take(flattened, pixels, axis=2).astype(jnp.float32)
    predicted = obs_operator(picked)
    centre = jnp.mean(predicted, axis=0)
    spread_rows = (predicted - centre) * incoming[1]
    misfit = (incoming[0] - centre) * incoming[1]
    obs_row = (pixels // tile_cols).astype(jnp.float32)
    obs_col = (pixels % tile_cols).astype(jnp.float32)
    packed = jnp.concatenate(
        [spread_rows, misfit[None], obs_row[None], obs_col[None]], axis=0
    ).astype(jnp.bfloat16)
    own_radius = lax.dynamic_slice(
        radius, (row_index * point_rows, col_index * point_cols), (point_rows, point_cols)
    ).astype(jnp.float32)
    beside_all = with_halo(packed[None, None], (("gy", 0), ("gx", 1)), 1)
    weighted_rows = beside_all[:, :, : members + 1, :]
    spreads = beside_all[:, :, :members, :]
    near_rows = (
        beside_all[:, :, members + 1, :].astype(jnp.float32)
        + ((jnp.arange(3) - 1) * tile_rows).astype(jnp.float32)[:, None, None]
    )
    near_cols = (
        beside_all[:, :, members + 2, :].astype(jnp.float32)
        + ((jnp.arange(3) - 1) * tile_cols).astype(jnp.float32)[None, :, None]
    )
    gram_list = []
    for point_col in range(point_cols):
        nearness = taper_weight(
            near_rows - half_step,
            near_cols - (stride * point_col + half_step),
            own_radius[0, point_col],
        )
        scaled = (nearness[:, :, None, :] * weighted_rows).astype(jnp.bfloat16)
        gram_list.append(
            jnp.einsum("abis,abjs->ij", scaled, spreads, preferred_element_type=jnp.float32)
        )
    gram_sum = jnp.stack(gram_list).reshape(point_rows, point_cols, members + 1, members)
    weights = solve_weights(gram_sum, members)
    framed = with_halo(
        weights.reshape(point_rows, point_cols, members * members), (("gy", 0), ("gx", 1)), 1
    )
    framed = framed.at[0].set(jnp.where(row_index == 0, framed[1], framed[0]))
    framed = framed.at[point_rows + 1].set(
        jnp.where(row_index == row_devices - 1, framed[point_rows], framed[point_rows + 1])
    )
    framed = framed.at[:, 0].set(jnp.where(col_index == 0, framed[:, 1], framed[:, 0]))
    framed = framed.at[:, point_cols + 1].set(
        jnp.where(col_index == col_devices - 1, framed[:, point_cols], framed[:, point_cols + 1])
    )
    framed = framed.reshape(point_rows + 2, point_cols + 2, members, members)
    centre_state = jnp.mean(state, axis=1, dtype=jnp.float32)
    anomaly = (state.astype(jnp.float32) - centre_state[:, None]).astype(jnp.bfloat16)
    pieces = anomaly.reshape(fields, members, 2 * point_rows, half_step, 2 * point_cols, half_step)
    upper_index = (np.arange(2 * point_rows) + 1) // 2
    left_index = (np.arange(2 * point_cols) + 1) // 2
    row_fraction = jnp.asarray(
        ((np.arange(tile_rows) + half_step) % stride / stride)
        .astype(np.float32)
        .reshape(2 * point_rows, half_step)
    )
    col_fraction = jnp.asarray(
        ((np.arange(tile_cols) + half_step) % stride / stride)
        .astype(np.float32)
        .reshape(2 * point_cols, half_step)
    )
    analysis = centre_state.reshape(fields, 1, 2 * point_rows, half_step, 2 * point_cols, half_step)
    for down_step in (0, 1):
        for right_step in (0, 1):
            corner = framed[upper_index + down_step][:, left_index + right_step]
            product = jnp.einsum(
                "fkhasb,hskm->fmhasb", pieces, corner, preferred_element_type=jnp.float32
            )
            row_weight = row_fraction if down_step else 1.0 - row_fraction
            col_weight = col_fraction if right_step else 1.0 - col_fraction
            blend = row_weight[:, :, None, None] * col_weight[None, None]
            analysis = analysis + blend * product
    return analysis.reshape(fields, members, tile_rows, tile_cols).astype(jnp.bfloat16)


MEMBERS = 64
ROWS = 32
COLS = 128
POINTS = 4
CAPACITY = 2 * OBS_PEER
PACK = 80
NT = (((1,), (1,)), ((), ()))
NN = (((1,), (0,)), ((), ()))


def dot(a, b, dims=NN, precision=None):
    return lax.dot_general(
        a, b, dims, precision=precision, preferred_element_type=jnp.float32
    )


def iota(shape, dim):
    return lax.broadcasted_iota(jnp.int32, shape, dim)


def split_high_low(x):
    high = x.astype(jnp.bfloat16)
    low = (x - high.astype(jnp.float32)).astype(jnp.bfloat16)
    return high, low


def pair_matmul(a, b, block_mask):
    a_high, a_low = split_high_low(a)
    diagonal = jnp.where(block_mask, jnp.concatenate([b, b], axis=0), 0.0)
    b_high, b_low = split_high_low(diagonal)
    return dot(a_high, b_high) + (dot(a_high, b_low) + dot(a_low, b_high))


def solve_pair(gram, forcing):
    shape = (MEMBERS, 2 * MEMBERS)
    identity = jnp.where(iota(shape, 0) == iota(shape, 1) % MEMBERS, 1.0, 0.0)
    square = (2 * MEMBERS, 2 * MEMBERS)
    block_mask = (iota(square, 0) < MEMBERS) == (iota(square, 1) < MEMBERS)
    left = iota((1, 2 * MEMBERS), 1) < MEMBERS
    matrix = identity + gram / (MEMBERS - 1.0)
    sums = jnp.sum(matrix * matrix, axis=0, keepdims=True)
    left_sum = jnp.sum(jnp.where(left, sums, 0.0), axis=1, keepdims=True)
    right_sum = jnp.sum(jnp.where(left, 0.0, sums), axis=1, keepdims=True)
    norm_scale = jnp.sqrt(jnp.where(left, left_sum, right_sum))
    current = matrix / norm_scale
    factor = 1.5 * identity - 0.5 * current
    inverse_root = factor
    current = pair_matmul(current, factor, block_mask)
    for iteration in range(1, ITER_NS):
        factor = 1.5 * identity - 0.5 * pair_matmul(inverse_root, current, block_mask)
        if iteration < ITER_NS - 1:
            current = pair_matmul(current, factor, block_mask)
        inverse_root = pair_matmul(factor, inverse_root, block_mask)
    square_root = inverse_root / jnp.sqrt(norm_scale)
    row = jnp.broadcast_to(forcing, (8, 2 * MEMBERS))
    shift = pair_matmul(pair_matmul(row, square_root, block_mask), square_root, block_mask)
    return (square_root + shift[0:1] / (MEMBERS - 1.0)).astype(jnp.bfloat16)


def kernel(
    peers,
    state_hbm, value_ref, sigma_ref, pixel_ref, route_ref, count_ref, radius_ref,
    out_hbm,
    state_v, wide, mixed, total, centres, outbox, inbox, picked, pack_own, pack_halo,
    weight_own, weight_halo, result,
    state_sem, out_sem, send_sem, recv_sem, pack_send, pack_recv, weight_send, weight_recv,
):
    group = lax.axis_index("groups")
    me = lax.axis_index("gy")
    fields = state_hbm.shape[0] // MEMBERS
    span = MEMBERS * ROWS

    def at(target):
        return (group, target, 0)

    load = pltpu.make_async_copy(state_hbm, state_v, state_sem)
    load.start()
    barrier = pltpu.get_barrier_semaphore()

    @pl.loop(1, peers)
    def _(step):
        pl.semaphore_signal(
            barrier, inc=1, device_id=at(lax.rem(me + step, peers)),
            device_id_type=pl.DeviceIdType.MESH,
        )

    arrivals = value_ref.shape[1]
    route = route_ref[...]
    present = iota((1, arrivals), 1) < count_ref[...]
    inverse_sigma = jnp.where(present, 1.0 / sigma_ref[...], 0.0)
    pixel = pixel_ref[...].astype(jnp.float32)
    kind = iota((8, arrivals), 0)
    record = jnp.where(
        kind == 0, value_ref[...],
        jnp.where(kind == 1, inverse_sigma, jnp.where(kind == 2, pixel, 0.0)),
    )
    hot = jnp.where(iota((peers, arrivals), 0) == route, 1.0, 0.0)
    earlier = jnp.where(iota((arrivals, arrivals), 0) < iota((arrivals, arrivals), 1), 1.0, 0.0)
    counted = dot(hot.astype(jnp.bfloat16), earlier.astype(jnp.bfloat16))
    rank = jnp.sum(counted * hot, axis=0, keepdims=True).astype(jnp.int32)
    place = jnp.where(iota((COLS, arrivals), 0) == rank + me * CAPACITY, 1.0, 0.0)
    routed = jnp.concatenate(
        [jnp.where(route == target, record, 0.0) for target in range(peers)], axis=0
    )
    outbox[...] = dot(routed, place, NT, lax.Precision.HIGHEST)
    own = pl.ds(pl.multiple_of(me * 8, 8), 8)

    @pl.when(me == 0)
    def _():
        pack_halo[0] = jnp.zeros((PACK, COLS), jnp.bfloat16)

    @pl.when(me == peers - 1)
    def _():
        pack_halo[1] = jnp.zeros((PACK, COLS), jnp.bfloat16)

    pl.semaphore_wait(barrier, peers - 1)

    def obs_copy(step):
        target = lax.rem(me + step, peers)
        return pltpu.make_async_remote_copy(
            src_ref=outbox.at[pl.ds(pl.multiple_of(target * 8, 8), 8)],
            dst_ref=inbox.at[own],
            send_sem=send_sem.at[step],
            recv_sem=recv_sem.at[step],
            device_id=at(target),
            device_id_type=pl.DeviceIdType.MESH,
        )

    @pl.loop(1, peers)
    def _(step):
        obs_copy(step).start()

    inbox[own, :] = outbox[own, :]
    load.wait()

    for field in range(fields):
        @pl.loop(0, 8)
        def _(chunk):
            first = pl.multiple_of(field * span + chunk * 256, 256)
            members = field * MEMBERS + chunk * 8
            wide[pl.ds(first, 256), :] = (
                state_v[pl.ds(members, 8)].astype(jnp.float32).reshape(256, COLS)
            )

    column = iota((1, COLS), 1)
    position = (column - STRIDE // 2).astype(jnp.float32) / STRIDE
    position = jnp.clip(position, 0.0, POINTS - 1.0)
    hats = [
        jnp.maximum(1.0 - jnp.abs(position - point), 0.0).astype(jnp.bfloat16)
        for point in range(POINTS)
    ]

    @pl.loop(0, ROWS)
    def _(row):
        for field in range(fields):
            cells = wide[pl.ds(field * span + row, MEMBERS, ROWS), :]
            centre = jnp.sum(cells, axis=0, keepdims=True) * (1.0 / MEMBERS)
            lanes = slice(field * COLS, (field + 1) * COLS)
            centres[row, :, lanes] = centre
            anomaly = (cells - centre).astype(jnp.bfloat16)
            for point in range(POINTS):
                mixed[row, point * MEMBERS:(point + 1) * MEMBERS, lanes] = anomaly * hats[point]

    @pl.loop(1, peers)
    def _(step):
        obs_copy(step).wait()

    arrived = jnp.sum(inbox[...].reshape(peers, 8, COLS), axis=0)
    value, weight = arrived[0:1], arrived[1:2]
    pixels = arrived[2:3].astype(jnp.int32)
    obs_row, obs_col = pixels // COLS, pixels % COLS
    col_hot = jnp.where(iota((COLS, COLS), 0) == obs_col, 1.0, 0.0).astype(jnp.bfloat16)
    row_hot = jnp.where(iota((ROWS, COLS), 0) == obs_row, 1.0, 0.0)
    for part in range(fields * 2):
        block = state_v[part * 32:(part + 1) * 32].reshape(32 * ROWS, COLS)
        found = dot(block, col_hot).reshape(32, ROWS, COLS) * row_hot
        picked[part * 32:(part + 1) * 32, :] = jnp.sum(found, axis=1)
    thickness, temperature, crust = (
        picked[field * MEMBERS:(field + 1) * MEMBERS, :] for field in range(fields)
    )
    predicted = temperature * jax.nn.sigmoid(thickness) - 0.5 * crust
    centre = jnp.mean(predicted, axis=0, keepdims=True)
    pack_own[0:MEMBERS, :] = ((predicted - centre) * weight).astype(jnp.bfloat16)
    kind = iota((PACK - MEMBERS, COLS), 0)
    pack_own[MEMBERS:PACK, :] = jnp.where(
        kind == 0, (value - centre) * weight,
        jnp.where(
            kind == 1, obs_row.astype(jnp.float32),
            jnp.where(kind == 2, obs_col.astype(jnp.float32), 0.0),
        ),
    ).astype(jnp.bfloat16)

    def halo_copy(source, slots, send, recv, down):
        return pltpu.make_async_remote_copy(
            src_ref=source,
            dst_ref=slots.at[0 if down else 1],
            send_sem=send.at[0 if down else 1],
            recv_sem=recv.at[0 if down else 1],
            device_id=at(me + 1 if down else me - 1),
            device_id_type=pl.DeviceIdType.MESH,
        )

    def exchange(source, slots, send, recv):
        @pl.when(me < peers - 1)
        def _():
            halo_copy(source, slots, send, recv, True).start()

        @pl.when(me > 0)
        def _():
            halo_copy(source, slots, send, recv, False).start()

    def finish(source, slots, send, recv):
        @pl.when(me < peers - 1)
        def _():
            halo_copy(source, slots, send, recv, True).wait_send()
            halo_copy(source, slots, send, recv, False).wait_recv()

        @pl.when(me > 0)
        def _():
            halo_copy(source, slots, send, recv, False).wait_send()
            halo_copy(source, slots, send, recv, True).wait_recv()

    exchange(pack_own, pack_halo, pack_send, pack_recv)
    radii = [radius_ref[me, point].astype(jnp.float32) for point in range(POINTS)]

    def tile_gram(pack, offset):
        spread = pack[0:MEMBERS]
        wider = pack.astype(jnp.float32)
        near_row = wider[MEMBERS + 1:MEMBERS + 2] + (offset * ROWS - STRIDE // 2)
        near_col = wider[MEMBERS + 2:MEMBERS + 3]
        scaled = []
        forced = []
        for point in range(POINTS):
            nearness = taper_weight(
                near_row, near_col - (STRIDE * point + STRIDE // 2), radii[point]
            )
            scaled.append((nearness * wider[0:MEMBERS]).astype(jnp.bfloat16))
            forced.append(nearness * wider[MEMBERS:MEMBERS + 1])
        forced = jnp.concatenate(forced + forced, axis=0).astype(jnp.bfloat16)
        gram = dot(spread, jnp.concatenate(scaled, axis=0), NT)
        forcing = dot(forced, jnp.concatenate([spread, spread], axis=0), NT)
        return gram, forcing

    gram, forcing = tile_gram(pack_own[...], 0)
    finish(pack_own, pack_halo, pack_send, pack_recv)
    for slot, offset in ((0, -1), (1, 1)):
        more_gram, more_forcing = tile_gram(pack_halo[slot], offset)
        gram, forcing = gram + more_gram, forcing + more_forcing
    left = iota((1, 2 * MEMBERS), 1) < MEMBERS
    for pair in range(POINTS // 2):
        lanes = slice(pair * 2 * MEMBERS, (pair + 1) * 2 * MEMBERS)
        rows = jnp.where(left, forcing[2 * pair:2 * pair + 1], forcing[2 * pair + 1:2 * pair + 2])
        weight_own[:, lanes] = solve_pair(gram[:, lanes], rows)
    exchange(weight_own, weight_halo, weight_send, weight_recv)

    half = ROWS // 2

    @pl.loop(0, ROWS)
    def _(row):
        fraction = (half + jnp.minimum(row, ROWS - row)).astype(jnp.float32) / STRIDE
        product = dot(weight_own[...], mixed[row])
        total[row] = centres[row] + fraction * product

    finish(weight_own, weight_halo, weight_send, weight_recv)

    @pl.when(me == 0)
    def _():
        weight_halo[0] = weight_own[...]

    @pl.when(me == peers - 1)
    def _():
        weight_halo[1] = weight_own[...]

    @pl.loop(0, ROWS)
    def _(row):
        fraction = (half - jnp.minimum(row, ROWS - row)).astype(jnp.float32) / STRIDE
        product = dot(weight_halo[row // half], mixed[row])
        done = total[row] + fraction * product
        for field in range(fields):
            wide[pl.ds(field * span + row, MEMBERS, ROWS), :] = (
                done[:, field * COLS:(field + 1) * COLS]
            )

    for field in range(fields):
        @pl.loop(0, 8)
        def _(chunk):
            first = pl.multiple_of(field * span + chunk * 256, 256)
            members = field * MEMBERS + chunk * 8
            result[pl.ds(members, 8)] = (
                wide[pl.ds(first, 256), :].astype(jnp.bfloat16).reshape(8, ROWS, COLS)
            )

    store = pltpu.make_async_copy(result, out_hbm, out_sem)
    store.start()
    store.wait()


def fused_body(state, obs_value, obs_sigma, obs_pixel, obs_route, obs_count, radius):
    fields, members, tile_rows, tile_cols = state.shape
    peers = lax.axis_size("gy")
    arrivals = obs_value.shape[0]
    planes = fields * members
    anywhere = pl.BlockSpec(memory_space=pl.ANY)
    local = pl.BlockSpec(memory_space=pltpu.VMEM)
    dma = pltpu.SemaphoreType.DMA
    analysis = pl.pallas_call(
        lambda *refs: kernel(peers, *refs),
        out_shape=jax.ShapeDtypeStruct((planes, tile_rows, tile_cols), jnp.bfloat16),
        in_specs=[anywhere] + [local] * 5 + [pl.BlockSpec(memory_space=pltpu.SMEM)],
        out_specs=anywhere,
        scratch_shapes=[
            pltpu.VMEM((planes, tile_rows, tile_cols), jnp.bfloat16),
            pltpu.VMEM((planes * tile_rows, tile_cols), jnp.float32),
            pltpu.VMEM((tile_rows, POINTS * members, fields * tile_cols), jnp.bfloat16),
            pltpu.VMEM((tile_rows, members, fields * tile_cols), jnp.float32),
            pltpu.VMEM((tile_rows, 1, fields * tile_cols), jnp.float32),
            pltpu.VMEM((peers * 8, tile_cols), jnp.float32),
            pltpu.VMEM((peers * 8, tile_cols), jnp.float32),
            pltpu.VMEM((planes, tile_cols), jnp.float32),
            pltpu.VMEM((PACK, tile_cols), jnp.bfloat16),
            pltpu.VMEM((2, PACK, tile_cols), jnp.bfloat16),
            pltpu.VMEM((members, POINTS * members), jnp.bfloat16),
            pltpu.VMEM((2, members, POINTS * members), jnp.bfloat16),
            pltpu.VMEM((planes, tile_rows, tile_cols), jnp.bfloat16),
            dma, dma, dma((peers,)), dma((peers,)), dma((2,)), dma((2,)), dma((2,)), dma((2,)),
        ],
        compiler_params=pltpu.CompilerParams(
            collective_id=0, has_side_effects=True, vmem_limit_bytes=40 * 1024 * 1024
        ),
    )(
        state.reshape(planes, tile_rows, tile_cols),
        obs_value.reshape(1, arrivals),
        obs_sigma.reshape(1, arrivals),
        obs_pixel.reshape(1, arrivals),
        obs_route.reshape(1, arrivals),
        obs_count.reshape(1, 1),
        radius,
    )
    return analysis.reshape(state.shape)


def solution(mesh):
    placed = (
        P("groups", None, "gy", "gx"),
        P(("groups", "gy", "gx")),
        P(("groups", "gy", "gx")),
        P(("groups", "gy", "gx")),
        P(("groups", "gy", "gx"), None),
        P(("groups", "gy", "gx")),
        P("groups", None),
    )
    slots = CAPACITY * mesh.shape["gy"]
    fits = mesh.shape["gx"] == 1 and slots == COLS
    return jax.shard_map(
        fused_body if fits else body, mesh=mesh, in_specs=placed, out_specs=P("groups", None, "gy", "gx"), check_vma=False
    )
```

```python
import jax
import jax.numpy as jnp
import numpy as np
from jax import lax
from jax.experimental import pallas as pl
from jax.experimental.pallas import tpu as pltpu
from jax.sharding import PartitionSpec as P

STRIDE = 32
ITER_NS = 6
OBS_PEER = 4


def with_halo(cells, sides, width):
    for axis, dim in sides:
        count = lax.axis_size(axis)
        ends = count - 1
        head = lax.slice_in_dim(cells, 0, width, axis=dim)
        tail = lax.slice_in_dim(cells, cells.shape[dim] - width, cells.shape[dim], axis=dim)
        cells = jnp.concatenate(
            [
                lax.ppermute(tail, axis, [(i, (i + 1) % count) for i in range(ends)]),
                cells,
                lax.ppermute(head, axis, [((i + 1) % count, i) for i in range(ends)]),
            ],
            axis=dim,
        )
    return cells


def obs_operator(values):
    return values[1] * jax.nn.sigmoid(values[0]) - 0.5 * values[2]


def taper_weight(row_offset, col_offset, own_radius):
    distance = row_offset * row_offset + col_offset * col_offset
    squared = own_radius * own_radius
    fraction = distance / squared
    return jnp.where(distance < squared, (1.0 - fraction) * (1.0 - fraction), 0.0)


def solve_weights(gram_matrix, members):
    spread = gram_matrix[..., :members, :]
    forcing = gram_matrix[..., members, :]
    identity = jnp.eye(members, dtype=jnp.float32)
    matrix = identity + spread / (members - 1.0)
    norm_scale = jnp.sqrt(jnp.sum(matrix * matrix, axis=(-2, -1), keepdims=True))
    current = matrix / norm_scale
    inverse_root = jnp.broadcast_to(identity, matrix.shape)
    for iteration in range(ITER_NS):
        factor = 1.5 * identity - 0.5 * jnp.matmul(
            inverse_root, current, precision=lax.Precision.HIGHEST
        )
        current = jnp.matmul(current, factor, precision=lax.Precision.HIGHEST)
        inverse_root = jnp.matmul(factor, inverse_root, precision=lax.Precision.HIGHEST)
    square_root = inverse_root / jnp.sqrt(norm_scale)
    pulled = jnp.einsum("...ij,...j->...i", square_root, forcing, precision=lax.Precision.HIGHEST)
    mean_shift = jnp.einsum(
        "...ij,...j->...i", square_root, pulled, precision=lax.Precision.HIGHEST
    ) / (members - 1.0)
    return (square_root + mean_shift[..., :, None]).astype(jnp.bfloat16)


def body(state, obs_value, obs_sigma, obs_pixel, obs_route, obs_count, radius):
    fields, members, tile_rows, tile_cols = state.shape
    row_devices = lax.axis_size("gy")
    col_devices = lax.axis_size("gx")
    row_index = lax.axis_index("gy")
    col_index = lax.axis_index("gx")
    stride = STRIDE
    half_step = stride // 2
    point_rows = tile_rows // stride
    point_cols = tile_cols // stride
    arrivals = obs_value.shape[0]
    capacity = 2 * OBS_PEER
    slot_count = capacity * row_devices
    present = jnp.arange(arrivals) < obs_count[0]
    inverse_sigma = jnp.where(present, 1.0 / obs_sigma, 0.0)
    target_row = obs_route[:, 0]
    one_hot = (target_row[:, None] == jnp.arange(row_devices)[None, :]).astype(jnp.int32)
    slot_rank = jnp.sum((jnp.cumsum(one_hot, axis=0) - one_hot) * one_hot, axis=1)
    placement = target_row * capacity + slot_rank
    record = jnp.stack([obs_value, inverse_sigma, obs_pixel.astype(jnp.float32)])
    outgoing = jnp.zeros((3, slot_count), jnp.float32).at[:, placement].set(record)
    incoming = lax.all_to_all(outgoing, "gy", split_axis=1, concat_axis=1, tiled=True)
    pixels = incoming[2].astype(jnp.int32)
    flattened = state.reshape(fields, members, tile_rows * tile_cols)
    picked = jnp.take(flattened, pixels, axis=2).astype(jnp.float32)
    predicted = obs_operator(picked)
    centre = jnp.mean(predicted, axis=0)
    spread_rows = (predicted - centre) * incoming[1]
    misfit = (incoming[0] - centre) * incoming[1]
    obs_row = (pixels // tile_cols).astype(jnp.float32)
    obs_col = (pixels % tile_cols).astype(jnp.float32)
    packed = jnp.concatenate(
        [spread_rows, misfit[None], obs_row[None], obs_col[None]], axis=0
    ).astype(jnp.bfloat16)
    own_radius = lax.dynamic_slice(
        radius, (row_index * point_rows, col_index * point_cols), (point_rows, point_cols)
    ).astype(jnp.float32)
    beside_all = with_halo(packed[None, None], (("gy", 0), ("gx", 1)), 1)
    weighted_rows = beside_all[:, :, : members + 1, :]
    spreads = beside_all[:, :, :members, :]
    near_rows = (
        beside_all[:, :, members + 1, :].astype(jnp.float32)
        + ((jnp.arange(3) - 1) * tile_rows).astype(jnp.float32)[:, None, None]
    )
    near_cols = (
        beside_all[:, :, members + 2, :].astype(jnp.float32)
        + ((jnp.arange(3) - 1) * tile_cols).astype(jnp.float32)[None, :, None]
    )
    gram_list = []
    for point_col in range(point_cols):
        nearness = taper_weight(
            near_rows - half_step,
            near_cols - (stride * point_col + half_step),
            own_radius[0, point_col],
        )
        scaled = (nearness[:, :, None, :] * weighted_rows).astype(jnp.bfloat16)
        gram_list.append(
            jnp.einsum("abis,abjs->ij", scaled, spreads, preferred_element_type=jnp.float32)
        )
    gram_sum = jnp.stack(gram_list).reshape(point_rows, point_cols, members + 1, members)
    weights = solve_weights(gram_sum, members)
    framed = with_halo(
        weights.reshape(point_rows, point_cols, members * members), (("gy", 0), ("gx", 1)), 1
    )
    framed = framed.at[0].set(jnp.where(row_index == 0, framed[1], framed[0]))
    framed = framed.at[point_rows + 1].set(
        jnp.where(row_index == row_devices - 1, framed[point_rows], framed[point_rows + 1])
    )
    framed = framed.at[:, 0].set(jnp.where(col_index == 0, framed[:, 1], framed[:, 0]))
    framed = framed.at[:, point_cols + 1].set(
        jnp.where(col_index == col_devices - 1, framed[:, point_cols], framed[:, point_cols + 1])
    )
    framed = framed.reshape(point_rows + 2, point_cols + 2, members, members)
    centre_state = jnp.mean(state, axis=1, dtype=jnp.float32)
    anomaly = (state.astype(jnp.float32) - centre_state[:, None]).astype(jnp.bfloat16)
    pieces = anomaly.reshape(fields, members, 2 * point_rows, half_step, 2 * point_cols, half_step)
    upper_index = (np.arange(2 * point_rows) + 1) // 2
    left_index = (np.arange(2 * point_cols) + 1) // 2
    row_fraction = jnp.asarray(
        ((np.arange(tile_rows) + half_step) % stride / stride)
        .astype(np.float32)
        .reshape(2 * point_rows, half_step)
    )
    col_fraction = jnp.asarray(
        ((np.arange(tile_cols) + half_step) % stride / stride)
        .astype(np.float32)
        .reshape(2 * point_cols, half_step)
    )
    analysis = centre_state.reshape(fields, 1, 2 * point_rows, half_step, 2 * point_cols, half_step)
    for down_step in (0, 1):
        for right_step in (0, 1):
            corner = framed[upper_index + down_step][:, left_index + right_step]
            product = jnp.einsum(
                "fkhasb,hskm->fmhasb", pieces, corner, preferred_element_type=jnp.float32
            )
            row_weight = row_fraction if down_step else 1.0 - row_fraction
            col_weight = col_fraction if right_step else 1.0 - col_fraction
            blend = row_weight[:, :, None, None] * col_weight[None, None]
            analysis = analysis + blend * product
    return analysis.reshape(fields, members, tile_rows, tile_cols).astype(jnp.bfloat16)


MEMBERS = 64
ROWS = 32
COLS = 128
POINTS = 4
CAPACITY = 2 * OBS_PEER
PACK = 80
NT = (((1,), (1,)), ((), ()))
NN = (((1,), (0,)), ((), ()))


def dot(a, b, dims=NN, precision=None):
    return lax.dot_general(
        a, b, dims, precision=precision, preferred_element_type=jnp.float32
    )


def iota(shape, dim):
    return lax.broadcasted_iota(jnp.int32, shape, dim)


def split_high_low(x):
    high = x.astype(jnp.bfloat16)
    low = (x - high.astype(jnp.float32)).astype(jnp.bfloat16)
    return high, low


def pair_matmul(a, b, block_mask):
    a_high, a_low = split_high_low(a)
    diagonal = jnp.where(block_mask, jnp.concatenate([b, b], axis=0), 0.0)
    b_high, b_low = split_high_low(diagonal)
    return dot(a_high, b_high) + (dot(a_high, b_low) + dot(a_low, b_high))


def solve_pair(gram, forcing):
    shape = (MEMBERS, 2 * MEMBERS)
    identity = jnp.where(iota(shape, 0) == iota(shape, 1) % MEMBERS, 1.0, 0.0)
    square = (2 * MEMBERS, 2 * MEMBERS)
    block_mask = (iota(square, 0) < MEMBERS) == (iota(square, 1) < MEMBERS)
    left = iota((1, 2 * MEMBERS), 1) < MEMBERS
    matrix = identity + gram / (MEMBERS - 1.0)
    sums = jnp.sum(matrix * matrix, axis=0, keepdims=True)
    left_sum = jnp.sum(jnp.where(left, sums, 0.0), axis=1, keepdims=True)
    right_sum = jnp.sum(jnp.where(left, 0.0, sums), axis=1, keepdims=True)
    norm_scale = jnp.sqrt(jnp.where(left, left_sum, right_sum))
    current = matrix / norm_scale
    factor = 1.5 * identity - 0.5 * current
    inverse_root = factor
    current = pair_matmul(current, factor, block_mask)
    for iteration in range(1, ITER_NS):
        factor = 1.5 * identity - 0.5 * pair_matmul(inverse_root, current, block_mask)
        if iteration < ITER_NS - 1:
            current = pair_matmul(current, factor, block_mask)
        inverse_root = pair_matmul(factor, inverse_root, block_mask)
    square_root = inverse_root / jnp.sqrt(norm_scale)
    row = jnp.broadcast_to(forcing, (8, 2 * MEMBERS))
    shift = pair_matmul(pair_matmul(row, square_root, block_mask), square_root, block_mask)
    return (square_root + shift[0:1] / (MEMBERS - 1.0)).astype(jnp.bfloat16)


def kernel(
    peers,
    state_hbm, value_hbm, sigma_hbm, pixel_hbm, route_hbm, count_hbm, radius_hbm,
    out_hbm,
    value_ref, sigma_ref, pixel_ref, route_ref, count_ref, radius_ref, small_sem,
    state_v, wide, mixed, total, centres, outbox, inbox, picked, pack_own, pack_halo,
    weight_own, weight_halo, result,
    state_sem, out_sem, send_sem, recv_sem, pack_send, pack_recv, weight_send, weight_recv,
):
    group = lax.axis_index("groups")
    me = lax.axis_index("gy")
    fields = state_hbm.shape[0] // MEMBERS
    span = MEMBERS * ROWS

    def at(target):
        return (group, target, 0)

    load = pltpu.make_async_copy(state_hbm, state_v, state_sem)
    small = [
        pltpu.make_async_copy(source, target, small_sem.at[index])
        for index, (source, target) in enumerate((
            (value_hbm, value_ref), (sigma_hbm, sigma_ref), (pixel_hbm, pixel_ref),
            (route_hbm, route_ref), (count_hbm, count_ref), (radius_hbm, radius_ref),
        ))
    ]
    for copy in small:
        copy.start()
    load.start()
    barrier = pltpu.get_barrier_semaphore()

    @pl.loop(1, peers)
    def _(step):
        pl.semaphore_signal(
            barrier, inc=1, device_id=at(lax.rem(me + step, peers)),
            device_id_type=pl.DeviceIdType.MESH,
        )

    for copy in small:
        copy.wait()
    arrivals = value_ref.shape[1]
    route = route_ref[...]
    present = iota((1, arrivals), 1) < count_ref[...]
    inverse_sigma = jnp.where(present, 1.0 / sigma_ref[...], 0.0)
    pixel = pixel_ref[...].astype(jnp.float32)
    kind = iota((8, arrivals), 0)
    record = jnp.where(
        kind == 0, value_ref[...],
        jnp.where(kind == 1, inverse_sigma, jnp.where(kind == 2, pixel, 0.0)),
    )
    hot = jnp.where(iota((peers, arrivals), 0) == route, 1.0, 0.0)
    earlier = jnp.where(iota((arrivals, arrivals), 0) < iota((arrivals, arrivals), 1), 1.0, 0.0)
    counted = dot(hot.astype(jnp.bfloat16), earlier.astype(jnp.bfloat16))
    rank = jnp.sum(counted * hot, axis=0, keepdims=True).astype(jnp.int32)
    place = jnp.where(iota((COLS, arrivals), 0) == rank + me * CAPACITY, 1.0, 0.0)
    routed = jnp.concatenate(
        [jnp.where(route == target, record, 0.0) for target in range(peers)], axis=0
    )
    outbox[...] = dot(routed, place, NT, lax.Precision.HIGHEST)
    own = pl.ds(pl.multiple_of(me * 8, 8), 8)

    @pl.when(me == 0)
    def _():
        pack_halo[0] = jnp.zeros((PACK, COLS), jnp.bfloat16)

    @pl.when(me == peers - 1)
    def _():
        pack_halo[1] = jnp.zeros((PACK, COLS), jnp.bfloat16)

    load.wait()

    for field in range(fields):
        @pl.loop(0, 8, unroll=2)
        def _(chunk):
            first = pl.multiple_of(field * span + chunk * 256, 256)
            members = field * MEMBERS + chunk * 8
            wide[pl.ds(first, 256), :] = (
                state_v[pl.ds(members, 8)].astype(jnp.float32).reshape(256, COLS)
            )

    pl.semaphore_wait(barrier, peers - 1)

    def obs_copy(step):
        target = lax.rem(me + step, peers)
        return pltpu.make_async_remote_copy(
            src_ref=outbox.at[pl.ds(pl.multiple_of(target * 8, 8), 8)],
            dst_ref=inbox.at[own],
            send_sem=send_sem.at[step],
            recv_sem=recv_sem.at[step],
            device_id=at(target),
            device_id_type=pl.DeviceIdType.MESH,
        )

    @pl.loop(1, peers)
    def _(step):
        obs_copy(step).start()

    inbox[own, :] = outbox[own, :]

    column = iota((1, COLS), 1)
    position = (column - STRIDE // 2).astype(jnp.float32) / STRIDE
    position = jnp.clip(position, 0.0, POINTS - 1.0)
    hats = [
        jnp.maximum(1.0 - jnp.abs(position - point), 0.0).astype(jnp.bfloat16)
        for point in range(POINTS)
    ]

    def mix(row):
        for field in range(fields):
            cells = wide[pl.ds(field * span + row, MEMBERS, ROWS), :]
            centre = jnp.sum(cells, axis=0, keepdims=True) * (1.0 / MEMBERS)
            lanes = slice(field * COLS, (field + 1) * COLS)
            centres[row, :, lanes] = centre
            anomaly = (cells - centre).astype(jnp.bfloat16)
            for point in range(POINTS):
                mixed[row, point * MEMBERS:(point + 1) * MEMBERS, lanes] = anomaly * hats[point]

    pl.loop(0, ROWS // 2, unroll=4)(mix)

    @pl.loop(1, peers)
    def _(step):
        obs_copy(step).wait()

    arrived = jnp.sum(inbox[...].reshape(peers, 8, COLS), axis=0)
    value, weight = arrived[0:1], arrived[1:2]
    pixels = arrived[2:3].astype(jnp.int32)
    obs_row, obs_col = pixels // COLS, pixels % COLS
    col_hot = jnp.where(iota((COLS, COLS), 0) == obs_col, 1.0, 0.0).astype(jnp.bfloat16)
    row_hot = jnp.where(iota((ROWS, COLS), 0) == obs_row, 1.0, 0.0)
    for part in range(fields * 2):
        block = state_v[part * 32:(part + 1) * 32].reshape(32 * ROWS, COLS)
        found = dot(block, col_hot).reshape(32, ROWS, COLS) * row_hot
        picked[part * 32:(part + 1) * 32, :] = jnp.sum(found, axis=1)
    thickness, temperature, crust = (
        picked[field * MEMBERS:(field + 1) * MEMBERS, :] for field in range(fields)
    )
    predicted = temperature * jax.nn.sigmoid(thickness) - 0.5 * crust
    centre = jnp.mean(predicted, axis=0, keepdims=True)
    pack_own[0:MEMBERS, :] = ((predicted - centre) * weight).astype(jnp.bfloat16)
    kind = iota((PACK - MEMBERS, COLS), 0)
    pack_own[MEMBERS:PACK, :] = jnp.where(
        kind == 0, (value - centre) * weight,
        jnp.where(
            kind == 1, obs_row.astype(jnp.float32),
            jnp.where(kind == 2, obs_col.astype(jnp.float32), 0.0),
        ),
    ).astype(jnp.bfloat16)

    def halo_copy(source, slots, send, recv, down):
        return pltpu.make_async_remote_copy(
            src_ref=source,
            dst_ref=slots.at[0 if down else 1],
            send_sem=send.at[0 if down else 1],
            recv_sem=recv.at[0 if down else 1],
            device_id=at(me + 1 if down else me - 1),
            device_id_type=pl.DeviceIdType.MESH,
        )

    def exchange(source, slots, send, recv):
        @pl.when(me < peers - 1)
        def _():
            halo_copy(source, slots, send, recv, True).start()

        @pl.when(me > 0)
        def _():
            halo_copy(source, slots, send, recv, False).start()

    def finish(source, slots, send, recv):
        @pl.when(me < peers - 1)
        def _():
            halo_copy(source, slots, send, recv, True).wait_send()
            halo_copy(source, slots, send, recv, False).wait_recv()

        @pl.when(me > 0)
        def _():
            halo_copy(source, slots, send, recv, False).wait_send()
            halo_copy(source, slots, send, recv, True).wait_recv()

    exchange(pack_own, pack_halo, pack_send, pack_recv)
    own_column = iota(radius_ref.shape, 1) == me
    radii = jnp.sum(jnp.where(own_column, radius_ref[...].astype(jnp.float32), 0.0), axis=1, keepdims=True)
    point_col = (iota((POINTS, 1), 0) * STRIDE + STRIDE // 2).astype(jnp.float32)

    def tile_gram(pack, offset):
        spread = pack[0:MEMBERS]
        wider = pack.astype(jnp.float32)
        near_row = wider[MEMBERS + 1:MEMBERS + 2] + (offset * ROWS - STRIDE // 2)
        near_col = wider[MEMBERS + 2:MEMBERS + 3]
        nearness = taper_weight(near_row, near_col - point_col, radii)
        scaled = [
            (nearness[point:point + 1] * wider[0:MEMBERS]).astype(jnp.bfloat16)
            for point in range(POINTS)
        ]
        forced = nearness * wider[MEMBERS:MEMBERS + 1]
        forced = jnp.concatenate([forced, forced], axis=0).astype(jnp.bfloat16)
        gram = dot(spread, jnp.concatenate(scaled, axis=0), NT)
        forcing = dot(forced, jnp.concatenate([spread, spread], axis=0), NT)
        return gram, forcing

    gram, forcing = tile_gram(pack_own[...], 0)
    pl.loop(ROWS // 2, ROWS, unroll=4)(mix)
    finish(pack_own, pack_halo, pack_send, pack_recv)
    for slot, offset in ((0, -1), (1, 1)):
        more_gram, more_forcing = tile_gram(pack_halo[slot], offset)
        gram, forcing = gram + more_gram, forcing + more_forcing
    left = iota((1, 2 * MEMBERS), 1) < MEMBERS
    for pair in range(POINTS // 2):
        lanes = slice(pair * 2 * MEMBERS, (pair + 1) * 2 * MEMBERS)
        rows = jnp.where(left, forcing[2 * pair:2 * pair + 1], forcing[2 * pair + 1:2 * pair + 2])
        weight_own[:, lanes] = solve_pair(gram[:, lanes], rows)
    exchange(weight_own, weight_halo, weight_send, weight_recv)

    half = ROWS // 2

    @pl.loop(0, ROWS, unroll=4)
    def _(row):
        fraction = (half + jnp.minimum(row, ROWS - row)).astype(jnp.float32) / STRIDE
        product = dot(weight_own[...], mixed[row])
        total[row] = centres[row] + fraction * product

    finish(weight_own, weight_halo, weight_send, weight_recv)

    @pl.when(me == 0)
    def _():
        weight_halo[0] = weight_own[...]

    @pl.when(me == peers - 1)
    def _():
        weight_halo[1] = weight_own[...]

    @pl.loop(0, ROWS, unroll=4)
    def _(row):
        fraction = (half - jnp.minimum(row, ROWS - row)).astype(jnp.float32) / STRIDE
        product = dot(weight_halo[row // half], mixed[row])
        done = total[row] + fraction * product
        for field in range(fields):
            wide[pl.ds(field * span + row, MEMBERS, ROWS), :] = (
                done[:, field * COLS:(field + 1) * COLS]
            )

    copies = [
        pltpu.make_async_copy(
            result.at[pl.ds(field * MEMBERS, MEMBERS)],
            out_hbm.at[pl.ds(field * MEMBERS, MEMBERS)],
            out_sem.at[field],
        )
        for field in range(fields)
    ]
    for field in range(fields):
        @pl.loop(0, 8, unroll=2)
        def _(chunk):
            first = pl.multiple_of(field * span + chunk * 256, 256)
            members = field * MEMBERS + chunk * 8
            result[pl.ds(members, 8)] = (
                wide[pl.ds(first, 256), :].astype(jnp.bfloat16).reshape(8, ROWS, COLS)
            )

        copies[field].start()

    for copy in copies:
        copy.wait()


def fused_body(state, obs_value, obs_sigma, obs_pixel, obs_route, obs_count, radius):
    fields, members, tile_rows, tile_cols = state.shape
    peers = lax.axis_size("gy")
    arrivals = obs_value.shape[0]
    planes = fields * members
    anywhere = pl.BlockSpec(memory_space=pl.ANY)
    dma = pltpu.SemaphoreType.DMA
    analysis = pl.pallas_call(
        lambda *refs: kernel(peers, *refs),
        out_shape=jax.ShapeDtypeStruct((planes, tile_rows, tile_cols), jnp.bfloat16),
        in_specs=[pl.BlockSpec(memory_space=pltpu.HBM)] * 7,
        out_specs=anywhere,
        scratch_shapes=[
            pltpu.VMEM((1, arrivals), jnp.float32),
            pltpu.VMEM((1, arrivals), jnp.float32),
            pltpu.VMEM((1, arrivals), jnp.int32),
            pltpu.VMEM((1, arrivals), jnp.int32),
            pltpu.VMEM((1, 1), jnp.int32),
            pltpu.VMEM(radius.shape[::-1], jnp.int32),
            dma((6,)),
            pltpu.VMEM((planes, tile_rows, tile_cols), jnp.bfloat16),
            pltpu.VMEM((planes * tile_rows, tile_cols), jnp.float32),
            pltpu.VMEM((tile_rows, POINTS * members, fields * tile_cols), jnp.bfloat16),
            pltpu.VMEM((tile_rows, members, fields * tile_cols), jnp.float32),
            pltpu.VMEM((tile_rows, 1, fields * tile_cols), jnp.float32),
            pltpu.VMEM((peers * 8, tile_cols), jnp.float32),
            pltpu.VMEM((peers * 8, tile_cols), jnp.float32),
            pltpu.VMEM((planes, tile_cols), jnp.float32),
            pltpu.VMEM((PACK, tile_cols), jnp.bfloat16),
            pltpu.VMEM((2, PACK, tile_cols), jnp.bfloat16),
            pltpu.VMEM((members, POINTS * members), jnp.bfloat16),
            pltpu.VMEM((2, members, POINTS * members), jnp.bfloat16),
            pltpu.VMEM((planes, tile_rows, tile_cols), jnp.bfloat16),
            dma, dma((fields,)), dma((peers,)), dma((peers,)), dma((2,)), dma((2,)), dma((2,)), dma((2,)),
        ],
        compiler_params=pltpu.CompilerParams(
            collective_id=0, has_side_effects=True, vmem_limit_bytes=63 * 1024 * 1024
        ),
    )(
        state.reshape(planes, tile_rows, tile_cols),
        obs_value.reshape(1, arrivals),
        obs_sigma.reshape(1, arrivals),
        obs_pixel.reshape(1, arrivals),
        obs_route.reshape(1, arrivals),
        obs_count.reshape(1, 1),
        radius.T,
    )
    return analysis.reshape(state.shape)


def solution(mesh):
    placed = (
        P("groups", None, "gy", "gx"),
        P(("groups", "gy", "gx")),
        P(("groups", "gy", "gx")),
        P(("groups", "gy", "gx")),
        P(("groups", "gy", "gx"), None),
        P(("groups", "gy", "gx")),
        P("groups", None),
    )
    slots = CAPACITY * mesh.shape["gy"]
    fits = mesh.shape["gx"] == 1 and slots == COLS
    return jax.shard_map(
        fused_body if fits else body, mesh=mesh, in_specs=placed, out_specs=P("groups", None, "gy", "gx"), check_vma=False
    )
```

```python
import jax
import jax.numpy as jnp
import numpy as np
from jax import lax
from jax.experimental import pallas as pl
from jax.experimental.pallas import tpu as pltpu
from jax.sharding import PartitionSpec as P

STRIDE = 32
ITER_NS = 6
OBS_PEER = 4


def with_halo(cells, sides, width):
    for axis, dim in sides:
        count = lax.axis_size(axis)
        ends = count - 1
        head = lax.slice_in_dim(cells, 0, width, axis=dim)
        tail = lax.slice_in_dim(cells, cells.shape[dim] - width, cells.shape[dim], axis=dim)
        cells = jnp.concatenate(
            [
                lax.ppermute(tail, axis, [(i, (i + 1) % count) for i in range(ends)]),
                cells,
                lax.ppermute(head, axis, [((i + 1) % count, i) for i in range(ends)]),
            ],
            axis=dim,
        )
    return cells


def obs_operator(values):
    return values[1] * jax.nn.sigmoid(values[0]) - 0.5 * values[2]


def taper_weight(row_offset, col_offset, own_radius):
    distance = row_offset * row_offset + col_offset * col_offset
    squared = own_radius * own_radius
    fraction = distance / squared
    return jnp.where(distance < squared, (1.0 - fraction) * (1.0 - fraction), 0.0)


def solve_weights(gram_matrix, members):
    spread = gram_matrix[..., :members, :]
    forcing = gram_matrix[..., members, :]
    identity = jnp.eye(members, dtype=jnp.float32)
    matrix = identity + spread / (members - 1.0)
    norm_scale = jnp.sqrt(jnp.sum(matrix * matrix, axis=(-2, -1), keepdims=True))
    current = matrix / norm_scale
    inverse_root = jnp.broadcast_to(identity, matrix.shape)
    for iteration in range(ITER_NS):
        factor = 1.5 * identity - 0.5 * jnp.matmul(
            inverse_root, current, precision=lax.Precision.HIGHEST
        )
        current = jnp.matmul(current, factor, precision=lax.Precision.HIGHEST)
        inverse_root = jnp.matmul(factor, inverse_root, precision=lax.Precision.HIGHEST)
    square_root = inverse_root / jnp.sqrt(norm_scale)
    pulled = jnp.einsum("...ij,...j->...i", square_root, forcing, precision=lax.Precision.HIGHEST)
    mean_shift = jnp.einsum(
        "...ij,...j->...i", square_root, pulled, precision=lax.Precision.HIGHEST
    ) / (members - 1.0)
    return (square_root + mean_shift[..., :, None]).astype(jnp.bfloat16)


def body(state, obs_value, obs_sigma, obs_pixel, obs_route, obs_count, radius):
    fields, members, tile_rows, tile_cols = state.shape
    row_devices = lax.axis_size("gy")
    col_devices = lax.axis_size("gx")
    row_index = lax.axis_index("gy")
    col_index = lax.axis_index("gx")
    stride = STRIDE
    half_step = stride // 2
    point_rows = tile_rows // stride
    point_cols = tile_cols // stride
    arrivals = obs_value.shape[0]
    capacity = 2 * OBS_PEER
    slot_count = capacity * row_devices
    present = jnp.arange(arrivals) < obs_count[0]
    inverse_sigma = jnp.where(present, 1.0 / obs_sigma, 0.0)
    target_row = obs_route[:, 0]
    one_hot = (target_row[:, None] == jnp.arange(row_devices)[None, :]).astype(jnp.int32)
    slot_rank = jnp.sum((jnp.cumsum(one_hot, axis=0) - one_hot) * one_hot, axis=1)
    placement = target_row * capacity + slot_rank
    record = jnp.stack([obs_value, inverse_sigma, obs_pixel.astype(jnp.float32)])
    outgoing = jnp.zeros((3, slot_count), jnp.float32).at[:, placement].set(record)
    incoming = lax.all_to_all(outgoing, "gy", split_axis=1, concat_axis=1, tiled=True)
    pixels = incoming[2].astype(jnp.int32)
    flattened = state.reshape(fields, members, tile_rows * tile_cols)
    picked = jnp.take(flattened, pixels, axis=2).astype(jnp.float32)
    predicted = obs_operator(picked)
    centre = jnp.mean(predicted, axis=0)
    spread_rows = (predicted - centre) * incoming[1]
    misfit = (incoming[0] - centre) * incoming[1]
    obs_row = (pixels // tile_cols).astype(jnp.float32)
    obs_col = (pixels % tile_cols).astype(jnp.float32)
    packed = jnp.concatenate(
        [spread_rows, misfit[None], obs_row[None], obs_col[None]], axis=0
    ).astype(jnp.bfloat16)
    own_radius = lax.dynamic_slice(
        radius, (row_index * point_rows, col_index * point_cols), (point_rows, point_cols)
    ).astype(jnp.float32)
    beside_all = with_halo(packed[None, None], (("gy", 0), ("gx", 1)), 1)
    weighted_rows = beside_all[:, :, : members + 1, :]
    spreads = beside_all[:, :, :members, :]
    near_rows = (
        beside_all[:, :, members + 1, :].astype(jnp.float32)
        + ((jnp.arange(3) - 1) * tile_rows).astype(jnp.float32)[:, None, None]
    )
    near_cols = (
        beside_all[:, :, members + 2, :].astype(jnp.float32)
        + ((jnp.arange(3) - 1) * tile_cols).astype(jnp.float32)[None, :, None]
    )
    gram_list = []
    for point_col in range(point_cols):
        nearness = taper_weight(
            near_rows - half_step,
            near_cols - (stride * point_col + half_step),
            own_radius[0, point_col],
        )
        scaled = (nearness[:, :, None, :] * weighted_rows).astype(jnp.bfloat16)
        gram_list.append(
            jnp.einsum("abis,abjs->ij", scaled, spreads, preferred_element_type=jnp.float32)
        )
    gram_sum = jnp.stack(gram_list).reshape(point_rows, point_cols, members + 1, members)
    weights = solve_weights(gram_sum, members)
    framed = with_halo(
        weights.reshape(point_rows, point_cols, members * members), (("gy", 0), ("gx", 1)), 1
    )
    framed = framed.at[0].set(jnp.where(row_index == 0, framed[1], framed[0]))
    framed = framed.at[point_rows + 1].set(
        jnp.where(row_index == row_devices - 1, framed[point_rows], framed[point_rows + 1])
    )
    framed = framed.at[:, 0].set(jnp.where(col_index == 0, framed[:, 1], framed[:, 0]))
    framed = framed.at[:, point_cols + 1].set(
        jnp.where(col_index == col_devices - 1, framed[:, point_cols], framed[:, point_cols + 1])
    )
    framed = framed.reshape(point_rows + 2, point_cols + 2, members, members)
    centre_state = jnp.mean(state, axis=1, dtype=jnp.float32)
    anomaly = (state.astype(jnp.float32) - centre_state[:, None]).astype(jnp.bfloat16)
    pieces = anomaly.reshape(fields, members, 2 * point_rows, half_step, 2 * point_cols, half_step)
    upper_index = (np.arange(2 * point_rows) + 1) // 2
    left_index = (np.arange(2 * point_cols) + 1) // 2
    row_fraction = jnp.asarray(
        ((np.arange(tile_rows) + half_step) % stride / stride)
        .astype(np.float32)
        .reshape(2 * point_rows, half_step)
    )
    col_fraction = jnp.asarray(
        ((np.arange(tile_cols) + half_step) % stride / stride)
        .astype(np.float32)
        .reshape(2 * point_cols, half_step)
    )
    analysis = centre_state.reshape(fields, 1, 2 * point_rows, half_step, 2 * point_cols, half_step)
    for down_step in (0, 1):
        for right_step in (0, 1):
            corner = framed[upper_index + down_step][:, left_index + right_step]
            product = jnp.einsum(
                "fkhasb,hskm->fmhasb", pieces, corner, preferred_element_type=jnp.float32
            )
            row_weight = row_fraction if down_step else 1.0 - row_fraction
            col_weight = col_fraction if right_step else 1.0 - col_fraction
            blend = row_weight[:, :, None, None] * col_weight[None, None]
            analysis = analysis + blend * product
    return analysis.reshape(fields, members, tile_rows, tile_cols).astype(jnp.bfloat16)


MEMBERS = 64
ROWS = 32
COLS = 128
POINTS = 4
CAPACITY = 2 * OBS_PEER
PACK = 80
NT = (((1,), (1,)), ((), ()))
NN = (((1,), (0,)), ((), ()))


def dot(a, b, dims=NN, precision=None):
    return lax.dot_general(
        a, b, dims, precision=precision, preferred_element_type=jnp.float32
    )


def iota(shape, dim):
    return lax.broadcasted_iota(jnp.int32, shape, dim)


def split_high_low(x):
    high = x.astype(jnp.bfloat16)
    low = (x - high.astype(jnp.float32)).astype(jnp.bfloat16)
    return high, low


def pair_matmul(a, b, block_mask):
    a_high, a_low = split_high_low(a)
    diagonal = jnp.where(block_mask, jnp.concatenate([b, b], axis=0), 0.0)
    b_high, b_low = split_high_low(diagonal)
    return dot(a_high, b_high) + (dot(a_high, b_low) + dot(a_low, b_high))


def solve_pair(gram, forcing):
    shape = (MEMBERS, 2 * MEMBERS)
    identity = jnp.where(iota(shape, 0) == iota(shape, 1) % MEMBERS, 1.0, 0.0)
    square = (2 * MEMBERS, 2 * MEMBERS)
    block_mask = (iota(square, 0) < MEMBERS) == (iota(square, 1) < MEMBERS)
    left = iota((1, 2 * MEMBERS), 1) < MEMBERS
    matrix = identity + gram / (MEMBERS - 1.0)
    sums = jnp.sum(matrix * matrix, axis=0, keepdims=True)
    left_sum = jnp.sum(jnp.where(left, sums, 0.0), axis=1, keepdims=True)
    right_sum = jnp.sum(jnp.where(left, 0.0, sums), axis=1, keepdims=True)
    norm_scale = jnp.sqrt(jnp.where(left, left_sum, right_sum))
    current = matrix / norm_scale
    factor = 1.5 * identity - 0.5 * current
    inverse_root = factor
    current = pair_matmul(current, factor, block_mask)
    yield
    for iteration in range(1, ITER_NS):
        factor = 1.5 * identity - 0.5 * pair_matmul(inverse_root, current, block_mask)
        yield
        if iteration < ITER_NS - 1:
            current = pair_matmul(current, factor, block_mask)
        inverse_root = pair_matmul(factor, inverse_root, block_mask)
        yield
    square_root = inverse_root / jnp.sqrt(norm_scale)
    row = jnp.broadcast_to(forcing, (8, 2 * MEMBERS))
    pulled = pair_matmul(row, square_root, block_mask)
    yield
    shift = pair_matmul(pulled, square_root, block_mask)
    yield (square_root + shift[0:1] / (MEMBERS - 1.0)).astype(jnp.bfloat16)


def kernel(
    peers,
    state_hbm, value_hbm, sigma_hbm, pixel_hbm, route_hbm, count_hbm, radius_hbm,
    out_hbm,
    value_ref, sigma_ref, pixel_ref, route_ref, count_ref, radius_ref, small_sem,
    state_v, wide, mixed, total, centres, outbox, inbox, picked, pack_own, pack_halo,
    weight_own, weight_halo, result,
    state_sem, out_sem, send_sem, recv_sem, pack_send, pack_recv, weight_send, weight_recv,
):
    group = lax.axis_index("groups")
    me = lax.axis_index("gy")
    fields = state_hbm.shape[0] // MEMBERS
    span = MEMBERS * ROWS

    def at(target):
        return (group, target, 0)

    load = pltpu.make_async_copy(state_hbm, state_v, state_sem)
    small = [
        pltpu.make_async_copy(source, target, small_sem.at[index])
        for index, (source, target) in enumerate((
            (value_hbm, value_ref), (sigma_hbm, sigma_ref), (pixel_hbm, pixel_ref),
            (route_hbm, route_ref), (count_hbm, count_ref), (radius_hbm, radius_ref),
        ))
    ]
    for copy in small:
        copy.start()
    load.start()
    barrier = pltpu.get_barrier_semaphore()

    @pl.loop(1, peers)
    def _(step):
        pl.semaphore_signal(
            barrier, inc=1, device_id=at(lax.rem(me + step, peers)),
            device_id_type=pl.DeviceIdType.MESH,
        )

    for copy in small:
        copy.wait()
    arrivals = value_ref.shape[1]
    route = route_ref[...]
    present = iota((1, arrivals), 1) < count_ref[...]
    inverse_sigma = jnp.where(present, 1.0 / sigma_ref[...], 0.0)
    pixel = pixel_ref[...].astype(jnp.float32)
    kind = iota((8, arrivals), 0)
    record = jnp.where(
        kind == 0, value_ref[...],
        jnp.where(kind == 1, inverse_sigma, jnp.where(kind == 2, pixel, 0.0)),
    )
    hot = jnp.where(iota((peers, arrivals), 0) == route, 1.0, 0.0)
    earlier = jnp.where(iota((arrivals, arrivals), 0) < iota((arrivals, arrivals), 1), 1.0, 0.0)
    counted = dot(hot.astype(jnp.bfloat16), earlier.astype(jnp.bfloat16))
    rank = jnp.sum(counted * hot, axis=0, keepdims=True).astype(jnp.int32)
    place = jnp.where(iota((COLS, arrivals), 0) == rank + me * CAPACITY, 1.0, 0.0)
    routed = jnp.concatenate(
        [jnp.where(route == target, record, 0.0) for target in range(peers)], axis=0
    )
    outbox[...] = dot(routed, place, NT, lax.Precision.HIGHEST)
    own = pl.ds(pl.multiple_of(me * 8, 8), 8)

    @pl.when(me == 0)
    def _():
        pack_halo[0] = jnp.zeros((PACK, COLS), jnp.bfloat16)

    @pl.when(me == peers - 1)
    def _():
        pack_halo[1] = jnp.zeros((PACK, COLS), jnp.bfloat16)

    load.wait()

    for field in range(fields):
        @pl.loop(0, 8, unroll=2)
        def _(chunk):
            first = pl.multiple_of(field * span + chunk * 256, 256)
            members = field * MEMBERS + chunk * 8
            wide[pl.ds(first, 256), :] = (
                state_v[pl.ds(members, 8)].astype(jnp.float32).reshape(256, COLS)
            )

    pl.semaphore_wait(barrier, peers - 1)

    def obs_copy(step):
        target = lax.rem(me + step, peers)
        return pltpu.make_async_remote_copy(
            src_ref=outbox.at[pl.ds(pl.multiple_of(target * 8, 8), 8)],
            dst_ref=inbox.at[own],
            send_sem=send_sem.at[step],
            recv_sem=recv_sem.at[step],
            device_id=at(target),
            device_id_type=pl.DeviceIdType.MESH,
        )

    @pl.loop(1, peers)
    def _(step):
        obs_copy(step).start()

    inbox[own, :] = outbox[own, :]

    column = iota((1, COLS), 1)
    position = (column - STRIDE // 2).astype(jnp.float32) / STRIDE
    position = jnp.clip(position, 0.0, POINTS - 1.0)
    hats = [
        jnp.maximum(1.0 - jnp.abs(position - point), 0.0).astype(jnp.bfloat16)
        for point in range(POINTS)
    ]

    def mix(row):
        for field in range(fields):
            cells = wide[pl.ds(field * span + row, MEMBERS, ROWS), :]
            centre = jnp.sum(cells, axis=0, keepdims=True) * (1.0 / MEMBERS)
            lanes = slice(field * COLS, (field + 1) * COLS)
            centres[row, :, lanes] = centre
            anomaly = (cells - centre).astype(jnp.bfloat16)
            for point in range(POINTS):
                mixed[row, point * MEMBERS:(point + 1) * MEMBERS, lanes] = anomaly * hats[point]

    pl.loop(0, ROWS // 2, unroll=4)(mix)

    @pl.loop(1, peers)
    def _(step):
        obs_copy(step).wait()

    arrived = jnp.sum(inbox[...].reshape(peers, 8, COLS), axis=0)
    value, weight = arrived[0:1], arrived[1:2]
    pixels = arrived[2:3].astype(jnp.int32)
    obs_row, obs_col = pixels // COLS, pixels % COLS
    col_hot = jnp.where(iota((COLS, COLS), 0) == obs_col, 1.0, 0.0).astype(jnp.bfloat16)
    row_hot = jnp.where(iota((ROWS, COLS), 0) == obs_row, 1.0, 0.0)
    for part in range(fields * 2):
        block = state_v[part * 32:(part + 1) * 32].reshape(32 * ROWS, COLS)
        found = dot(block, col_hot).reshape(32, ROWS, COLS) * row_hot
        picked[part * 32:(part + 1) * 32, :] = jnp.sum(found, axis=1)
    thickness, temperature, crust = (
        picked[field * MEMBERS:(field + 1) * MEMBERS, :] for field in range(fields)
    )
    predicted = temperature * jax.nn.sigmoid(thickness) - 0.5 * crust
    centre = jnp.mean(predicted, axis=0, keepdims=True)
    pack_own[0:MEMBERS, :] = ((predicted - centre) * weight).astype(jnp.bfloat16)
    kind = iota((PACK - MEMBERS, COLS), 0)
    pack_own[MEMBERS:PACK, :] = jnp.where(
        kind == 0, (value - centre) * weight,
        jnp.where(
            kind == 1, obs_row.astype(jnp.float32),
            jnp.where(kind == 2, obs_col.astype(jnp.float32), 0.0),
        ),
    ).astype(jnp.bfloat16)

    def halo_copy(source, slots, send, recv, down):
        return pltpu.make_async_remote_copy(
            src_ref=source,
            dst_ref=slots.at[0 if down else 1],
            send_sem=send.at[0 if down else 1],
            recv_sem=recv.at[0 if down else 1],
            device_id=at(me + 1 if down else me - 1),
            device_id_type=pl.DeviceIdType.MESH,
        )

    def exchange(source, slots, send, recv):
        @pl.when(me < peers - 1)
        def _():
            halo_copy(source, slots, send, recv, True).start()

        @pl.when(me > 0)
        def _():
            halo_copy(source, slots, send, recv, False).start()

    def finish(source, slots, send, recv):
        @pl.when(me < peers - 1)
        def _():
            halo_copy(source, slots, send, recv, True).wait_send()
            halo_copy(source, slots, send, recv, False).wait_recv()

        @pl.when(me > 0)
        def _():
            halo_copy(source, slots, send, recv, False).wait_send()
            halo_copy(source, slots, send, recv, True).wait_recv()

    exchange(pack_own, pack_halo, pack_send, pack_recv)
    own_column = iota(radius_ref.shape, 1) == me
    radii = jnp.sum(jnp.where(own_column, radius_ref[...].astype(jnp.float32), 0.0), axis=1, keepdims=True)
    point_col = (iota((POINTS, 1), 0) * STRIDE + STRIDE // 2).astype(jnp.float32)

    def tile_gram(pack, offset):
        spread = pack[0:MEMBERS]
        wider = pack.astype(jnp.float32)
        near_row = wider[MEMBERS + 1:MEMBERS + 2] + (offset * ROWS - STRIDE // 2)
        near_col = wider[MEMBERS + 2:MEMBERS + 3]
        nearness = taper_weight(near_row, near_col - point_col, radii)
        scaled = [
            (nearness[point:point + 1] * wider[0:MEMBERS]).astype(jnp.bfloat16)
            for point in range(POINTS)
        ]
        forced = nearness * wider[MEMBERS:MEMBERS + 1]
        forced = jnp.concatenate([forced, forced], axis=0).astype(jnp.bfloat16)
        gram = dot(spread, jnp.concatenate(scaled, axis=0), NT)
        forcing = dot(forced, jnp.concatenate([spread, spread], axis=0), NT)
        return gram, forcing

    gram, forcing = tile_gram(pack_own[...], 0)
    pl.loop(ROWS // 2, ROWS, unroll=4)(mix)
    finish(pack_own, pack_halo, pack_send, pack_recv)
    for slot, offset in ((0, -1), (1, 1)):
        more_gram, more_forcing = tile_gram(pack_halo[slot], offset)
        gram, forcing = gram + more_gram, forcing + more_forcing
    left = iota((1, 2 * MEMBERS), 1) < MEMBERS
    solvers = []
    for pair in range(POINTS // 2):
        lanes = slice(pair * 2 * MEMBERS, (pair + 1) * 2 * MEMBERS)
        rows = jnp.where(left, forcing[2 * pair:2 * pair + 1], forcing[2 * pair + 1:2 * pair + 2])
        solvers.append(solve_pair(gram[:, lanes], rows))
    for solved in zip(*solvers):
        pass
    weight_own[...] = jnp.concatenate(solved, axis=1)
    exchange(weight_own, weight_halo, weight_send, weight_recv)

    half = ROWS // 2

    @pl.loop(0, ROWS, unroll=4)
    def _(row):
        fraction = (half + jnp.minimum(row, ROWS - row)).astype(jnp.float32) / STRIDE
        product = dot(weight_own[...], mixed[row])
        total[row] = centres[row] + fraction * product

    finish(weight_own, weight_halo, weight_send, weight_recv)

    @pl.when(me == 0)
    def _():
        weight_halo[0] = weight_own[...]

    @pl.when(me == peers - 1)
    def _():
        weight_halo[1] = weight_own[...]

    @pl.loop(0, ROWS, unroll=4)
    def _(row):
        fraction = (half - jnp.minimum(row, ROWS - row)).astype(jnp.float32) / STRIDE
        product = dot(weight_halo[row // half], mixed[row])
        done = total[row] + fraction * product
        for field in range(fields):
            wide[pl.ds(field * span + row, MEMBERS, ROWS), :] = (
                done[:, field * COLS:(field + 1) * COLS]
            )

    copies = [
        pltpu.make_async_copy(
            result.at[pl.ds(field * MEMBERS, MEMBERS)],
            out_hbm.at[pl.ds(field * MEMBERS, MEMBERS)],
            out_sem.at[field],
        )
        for field in range(fields)
    ]
    for field in range(fields):
        @pl.loop(0, 8, unroll=2)
        def _(chunk):
            first = pl.multiple_of(field * span + chunk * 256, 256)
            members = field * MEMBERS + chunk * 8
            result[pl.ds(members, 8)] = (
                wide[pl.ds(first, 256), :].astype(jnp.bfloat16).reshape(8, ROWS, COLS)
            )

        copies[field].start()

    for copy in copies:
        copy.wait()


def fused_body(state, obs_value, obs_sigma, obs_pixel, obs_route, obs_count, radius):
    fields, members, tile_rows, tile_cols = state.shape
    peers = lax.axis_size("gy")
    arrivals = obs_value.shape[0]
    planes = fields * members
    anywhere = pl.BlockSpec(memory_space=pl.ANY)
    dma = pltpu.SemaphoreType.DMA
    analysis = pl.pallas_call(
        lambda *refs: kernel(peers, *refs),
        out_shape=jax.ShapeDtypeStruct((planes, tile_rows, tile_cols), jnp.bfloat16),
        in_specs=[pl.BlockSpec(memory_space=pltpu.HBM)] * 7,
        out_specs=anywhere,
        scratch_shapes=[
            pltpu.VMEM((1, arrivals), jnp.float32),
            pltpu.VMEM((1, arrivals), jnp.float32),
            pltpu.VMEM((1, arrivals), jnp.int32),
            pltpu.VMEM((1, arrivals), jnp.int32),
            pltpu.VMEM((1, 1), jnp.int32),
            pltpu.VMEM(radius.shape[::-1], jnp.int32),
            dma((6,)),
            pltpu.VMEM((planes, tile_rows, tile_cols), jnp.bfloat16),
            pltpu.VMEM((planes * tile_rows, tile_cols), jnp.float32),
            pltpu.VMEM((tile_rows, POINTS * members, fields * tile_cols), jnp.bfloat16),
            pltpu.VMEM((tile_rows, members, fields * tile_cols), jnp.float32),
            pltpu.VMEM((tile_rows, 1, fields * tile_cols), jnp.float32),
            pltpu.VMEM((peers * 8, tile_cols), jnp.float32),
            pltpu.VMEM((peers * 8, tile_cols), jnp.float32),
            pltpu.VMEM((planes, tile_cols), jnp.float32),
            pltpu.VMEM((PACK, tile_cols), jnp.bfloat16),
            pltpu.VMEM((2, PACK, tile_cols), jnp.bfloat16),
            pltpu.VMEM((members, POINTS * members), jnp.bfloat16),
            pltpu.VMEM((2, members, POINTS * members), jnp.bfloat16),
            pltpu.VMEM((planes, tile_rows, tile_cols), jnp.bfloat16),
            dma, dma((fields,)), dma((peers,)), dma((peers,)), dma((2,)), dma((2,)), dma((2,)), dma((2,)),
        ],
        compiler_params=pltpu.CompilerParams(
            collective_id=0, has_side_effects=True, vmem_limit_bytes=63 * 1024 * 1024
        ),
    )(
        state.reshape(planes, tile_rows, tile_cols),
        obs_value.reshape(1, arrivals),
        obs_sigma.reshape(1, arrivals),
        obs_pixel.reshape(1, arrivals),
        obs_route.reshape(1, arrivals),
        obs_count.reshape(1, 1),
        radius.T,
    )
    return analysis.reshape(state.shape)


def solution(mesh):
    placed = (
        P("groups", None, "gy", "gx"),
        P(("groups", "gy", "gx")),
        P(("groups", "gy", "gx")),
        P(("groups", "gy", "gx")),
        P(("groups", "gy", "gx"), None),
        P(("groups", "gy", "gx")),
        P("groups", None),
    )
    slots = CAPACITY * mesh.shape["gy"]
    fits = mesh.shape["gx"] == 1 and slots == COLS
    return jax.shard_map(
        fused_body if fits else body, mesh=mesh, in_specs=placed, out_specs=P("groups", None, "gy", "gx"), check_vma=False
    )
```
